256 devices in a mesh: dp: 256 (over x, y, z, core).
Axes of the slice: x: 4, y: 4, z: 8, core: 2. Of those that a mesh axis runs over, the one named last changes fastest.
Arguments:
- image_emb: float32 [65536, 1280], P('dp'), may hold values from -50 to 50
- text_emb: float32 [65536, 1280], P('dp'), may hold values from -50 to 50
- logit_scale: float32 [], replicated, may hold values from 2 to 4
Outputs:
- loss: float32 [], replicated
- image_grad: float32 [65536, 1280], P('dp')
- text_grad: float32 [65536, 1280], P('dp')
- scale_grad: float32 [], replicated
The draws below stay inside these ranges and needn't reach their ends.
All inputs are finite; a program needn't handle non-finite values.
Results may differ from the reference program's by a relative error of at most 0.0003.
Values sent between devices are 32-bit elements; how exact they have to be, the bound alone decides.
No kernel may reach another device: no remote copies, remote signals or barrier semaphores. Data moves between devices by JAX's collectives and lax.ppermute only.
A program may use at most 64 MiB of HBM per device.

```python
import math
from functools import reduce
import jax
import jax.numpy as jnp
from jax import lax

D = 1280
ROWS_DEV = 256
WIN = 8
LOOPLEN = 256
NROWS = 65536


def joint_pair(key):
    keys = jax.random.split(key, 2)
    shared_base = jax.random.normal(keys[0], (NROWS, D), jnp.float32)
    text_noise = jax.random.normal(keys[1], (NROWS, D), jnp.float32)
    row_index = jnp.arange(NROWS).astype(jnp.float32)
    pairing = 0.02 * (1.0 - row_index / NROWS)
    image_draw = shared_base * D ** (-0.5)
    text_draw = pairing[:, None] * shared_base + text_noise
    return (jnp.clip(image_draw, -50.0, 50.0), jnp.clip(text_draw, -50.0, 50.0))


def draw_image_emb(key, part):
    return joint_pair(key)[0]


def draw_text_emb(key, part):
    return joint_pair(key)[1]


def setup_inputs(seed: int = 0) -> dict:
    splits = jax.random.split(jax.random.key(seed), 4)
    return {
        "image_emb": draw_image_emb(jax.random.fold_in(splits[3], 71), 0),
        "text_emb": draw_text_emb(jax.random.fold_in(splits[3], 71), 0),
        "logit_scale": jnp.clip(jnp.exp(jax.random.uniform(splits[2], (), jnp.float32, math.log(2.0), math.log(4.0))), 2.0, 4.0),
    }


precise = lax.Precision.HIGHEST


def reference(image_emb, text_emb, logit_scale):
    lower_reach = WIN // 2 - 1
    image_rows = image_emb.reshape(LOOPLEN, ROWS_DEV, D)
    text_rows = text_emb.reshape(LOOPLEN, ROWS_DEV, D)
    offsets = [visit_index - lower_reach for visit_index in range(WIN)]
    logits = []
    for offset in offsets:
        partner = jnp.roll(text_rows, -offset, axis=0)
        logits.append(logit_scale * jnp.einsum("pbd,pcd->pbc", image_rows, partner, precision=precise))
    row_lse = reduce(jnp.logaddexp, [jax.nn.logsumexp(block_logits, axis=2) for block_logits in logits])
    col_lse = reduce(jnp.logaddexp, [jax.nn.logsumexp(jnp.roll(block_logits, offset, axis=0), axis=1) for block_logits, offset in zip(logits, offsets)])
    diagonal = jnp.diagonal(logits[lower_reach], axis1=1, axis2=2)
    loss_value = (jnp.sum(row_lse) + jnp.sum(col_lse) - 2.0 * jnp.sum(diagonal)) / (2.0 * NROWS)
    identity = jnp.eye(ROWS_DEV, dtype=jnp.float32)
    image_acc = jnp.zeros((LOOPLEN, ROWS_DEV, D), jnp.float32)
    text_acc = jnp.zeros((LOOPLEN, ROWS_DEV, D), jnp.float32)
    scale_sum = jnp.zeros((), jnp.float32)
    for block_logits, offset in zip(logits, offsets):
        col_here = jnp.roll(col_lse, -offset, axis=0)
        weights = jnp.exp(block_logits - row_lse[:, :, None]) + jnp.exp(block_logits - col_here[:, None, :])
        if offset == 0:
            weights = weights - 2.0 * identity
        partner = jnp.roll(text_rows, -offset, axis=0)
        image_acc = image_acc + jnp.einsum("pbc,pcd->pbd", weights, partner, precision=precise)
        text_acc = text_acc + jnp.roll(jnp.einsum("pbc,pbd->pcd", weights, image_rows, precision=precise), offset, axis=0)
        scale_sum = scale_sum + jnp.sum(weights * block_logits)
    half_scale = 0.5 * logit_scale
    image_grad = (half_scale * image_acc).reshape(NROWS, D)
    text_grad = (half_scale * text_acc).reshape(NROWS, D)
    scale_grad = scale_sum / (2.0 * NROWS * logit_scale)
    return (loss_value, image_grad, text_grad, scale_grad)
```

```python
import jax
import jax.numpy as jnp
from jax import lax
from jax.sharding import PartitionSpec as P

WIN = 8
BOTH = (0, 1)

highest = lax.Precision.HIGHEST
high = lax.Precision.HIGH


def shift(value, steps, cores=BOTH):
    count = lax.axis_size("dp")
    pairs = [(s, (s + steps) % count) for s in range(count) if s % 2 in cores]
    return lax.ppermute(value, "dp", pairs)


def swap(value):
    count = lax.axis_size("dp")
    return lax.ppermute(value, "dp", [(s, s ^ 1) for s in range(count)])


def scores(rows, block, scale):
    return scale * lax.dot_general(
        rows,
        block,
        (((1,), (1,)), ((), ())),
        precision=highest,
        preferred_element_type=jnp.float32,
    )


def apply(weights, block):
    return jnp.dot(weights, block, precision=high, preferred_element_type=jnp.float32)


def lse(logits, axis):
    top = jnp.max(logits, axis=axis, keepdims=True)
    total = jnp.sum(jnp.exp(logits - top), axis=axis)
    return jnp.squeeze(top, axis) + jnp.log(total)


def merge(parts):
    return lse(jnp.stack(parts), 0)


def on_device(image, text, scale):
    rows = image.shape[0]
    first = lax.axis_index("dp") % 2 == 0
    eye = jnp.eye(rows, dtype=jnp.float32)

    text_p = shift(text, 2)
    text_m = shift(text, -2)
    image_s = swap(image)
    text_mm = shift(text_m, -2)
    text_pp = shift(text_p, 2, (1,))
    text_s = swap(text)
    image_p = shift(image, 2)
    image_m = shift(image, -2)
    image_pp = shift(image_p, 2)
    image_mm = shift(image_m, -2, (0,))

    near_t = {-2: text_p, 0: text, 2: text_m}
    far_own_t = text_mm
    far_sib_t = jnp.where(first, text_mm, text_pp)
    both_i = jnp.concatenate([image, image_s])
    near_l = {b: scores(both_i, t, scale) for b, t in near_t.items()}
    own_l = scores(image, far_own_t, scale)
    sib_l = scores(image_s, far_sib_t, scale)

    row_own = merge([lse(v[:rows], 1) for v in near_l.values()] + [lse(own_l, 1)])
    row_sib = merge([lse(v[rows:], 1) for v in near_l.values()] + [lse(sib_l, 1)])
    got = swap(jnp.stack([row_own, row_sib]))
    row_lse = merge([row_own, got[1]])
    row_lse_s = merge([row_sib, got[0]])

    col_near = {b: lse(v, 0) for b, v in near_l.items()}
    col_own = lse(own_l, 0)
    col_sib = lse(sib_l, 0)
    col_far = jnp.where(first, merge([col_own, col_sib]), col_own)
    from_m = shift(col_near[2], 2)
    from_p = shift(col_near[-2], -2)
    from_mm = shift(col_far, 4)
    from_pp = shift(col_sib, -4, (1,))
    from_pp = jnp.where(first, -jnp.inf, from_pp)
    col_lse = merge([col_near[0], from_m, from_p, from_mm, from_pp])

    diagonal = jnp.diagonal(near_l[0][:rows])
    loss_part = jnp.sum(row_lse) + jnp.sum(col_lse) - 2.0 * jnp.sum(diagonal)

    mine = jnp.stack([row_lse, col_lse])
    at = {0: mine}
    for step in (2, -2, 4, -4):
        at[-step] = shift(mine, step)
    col_lse_s = swap(col_lse)

    row_both = jnp.concatenate([row_lse, row_lse_s])[:, None]
    image_acc = jnp.zeros((2 * rows, image.shape[1]), jnp.float32)
    scale_acc = jnp.zeros((), jnp.float32)
    zero = jnp.zeros_like(eye)
    corner = jnp.concatenate([2.0 * eye, zero])
    for b, t in near_t.items():
        v = near_l[b]
        w = jnp.exp(v - row_both) + jnp.exp(v - at[b][1][None, :])
        if b == 0:
            w = w - corner
        image_acc += apply(w, t)
        scale_acc += jnp.sum(w * v)
    w = jnp.exp(own_l - row_lse[:, None]) + jnp.exp(own_l - at[4][1][None, :])
    scale_acc += jnp.sum(w * own_l)
    image_own = image_acc[:rows] + apply(w, far_own_t)
    col_e = jnp.where(first, at[4][1], at[-4][1])
    w = jnp.exp(sib_l - row_lse_s[:, None]) + jnp.exp(sib_l - col_e[None, :])
    scale_acc += jnp.sum(w * sib_l)
    image_sib = image_acc[rows:] + apply(w, far_sib_t)
    image_grad = 0.5 * scale * (image_own + swap(image_sib))

    near_i = {-2: image_p, 0: image, 2: image_m}
    far_own_i = image_pp
    far_sib_i = jnp.where(first, image_mm, image_pp)
    both_t = jnp.concatenate([text, text_s])
    col_both = jnp.concatenate([col_lse, col_lse_s])[:, None]
    text_acc = jnp.zeros((2 * rows, image.shape[1]), jnp.float32)
    for b, i in near_i.items():
        v = scores(both_t, i, scale)
        w = jnp.exp(v - col_both) + jnp.exp(v - at[b][0][None, :])
        if b == 0:
            w = w - corner
        text_acc += apply(w, i)
    v = scores(text, far_own_i, scale)
    w = jnp.exp(v - col_lse[:, None]) + jnp.exp(v - at[-4][0][None, :])
    text_own = text_acc[:rows] + apply(w, far_own_i)
    v = scores(text_s, far_sib_i, scale)
    row_f = jnp.where(first, at[4][0], at[-4][0])
    w = jnp.exp(v - col_lse_s[:, None]) + jnp.exp(v - row_f[None, :])
    text_sib = text_acc[rows:] + apply(w, far_sib_i)
    text_grad = 0.5 * scale * (text_own + swap(text_sib))

    loss_total, scale_total = lax.psum((loss_part, scale_acc), "dp")
    total_rows = rows * lax.axis_size("dp")
    loss = loss_total / (2.0 * total_rows)
    scale_grad = scale_total / (2.0 * total_rows * scale)
    return (loss, image_grad, text_grad, scale_grad)


def solution(mesh):
    in_specs = (P("dp", None), P("dp", None), P())
    out_specs = (P(), P("dp", None), P("dp", None), P())
    return jax.shard_map(
        on_device, mesh=mesh, in_specs=in_specs, out_specs=out_specs, check_vma=False
    )
```

```python
import functools

import jax
import jax.numpy as jnp
from jax import lax
from jax.experimental import pallas as pl
from jax.experimental.pallas import tpu as pltpu
from jax.sharding import PartitionSpec as P

WIN = 8
BOTH = (0, 1)
LIMIT = 10 * 1024 * 1024
TILE = 256
F32 = jnp.float32
BF16 = jnp.bfloat16
VMEM = pl.BlockSpec(memory_space=pltpu.VMEM)
SMEM = pl.BlockSpec(memory_space=pltpu.SMEM)
ANY = pl.BlockSpec(memory_space=pl.ANY)


def shift(value, steps, cores=BOTH):
    count = lax.axis_size("dp")
    pairs = [(s, (s + steps) % count) for s in range(count) if s % 2 in cores]
    return lax.ppermute(value, "dp", pairs)


def swap(value, bit=1):
    count = lax.axis_size("dp")
    return lax.ppermute(value, "dp", [(s, s ^ bit) for s in range(count)])


def after(value, *done):
    return lax.optimization_barrier((value, done))[0]


def call(kernel, name, micros, outs, args, scratch=(), out_space=VMEM, alias=None):
    return pl.pallas_call(
        kernel,
        name=name,
        out_shape=[jax.ShapeDtypeStruct(s, d) for s, d in outs],
        in_specs=[SMEM] + [VMEM] * (len(args) - 1),
        out_specs=[out_space] * len(outs),
        scratch_shapes=[
            pltpu.VMEM(*x) if isinstance(x, tuple) else x for x in scratch
        ],
        compiler_params=pltpu.CompilerParams(vmem_limit_bytes=LIMIT),
        input_output_aliases=alias or {},
        cost_estimate=pl.CostEstimate(
            flops=int(micros * 1.15e9), bytes_accessed=1, transcendentals=0
        ),
    )(*args)


def dot_nt(a, b):
    return lax.dot_general(a, b, (((1,), (1,)), ((), ())), preferred_element_type=F32)


def dot_nn(a, b):
    return lax.dot_general(a, b, (((1,), (0,)), ((), ())), preferred_element_type=F32)


def two(x):
    h = x.astype(BF16)
    return h, (x - h.astype(F32)).astype(BF16)


def three(x):
    h = x.astype(BF16)
    r = x - h.astype(F32)
    m = r.astype(BF16)
    return h, m, (r - m.astype(F32)).astype(BF16)


def scores(a, b):
    (ah, am, al), (bh, bm, bl) = a, b
    small = dot_nt(ah, bl) + dot_nt(al, bh) + dot_nt(am, bm)
    return (small + (dot_nt(ah, bm) + dot_nt(am, bh))) + dot_nt(ah, bh)


def put_three(x, h, m, l):
    h[...], m[...], l[...] = three(x)


def take(refs, rows=slice(None)):
    return tuple(r[rows] for r in refs)


def column(v):
    return jnp.transpose(jnp.broadcast_to(v, (8, v.shape[1])))[:, :1]


def row(v):
    return jnp.transpose(jnp.broadcast_to(v, (v.shape[0], 128)))[:1]


def stat(tops, sums, means):
    top = functools.reduce(jnp.maximum, tops)
    total = sum(jnp.exp(t - top) * s for t, s in zip(tops, sums))
    mean = sum(jnp.exp(t - top) * m for t, m in zip(tops, means))
    return top + jnp.log(total), mean / total


def merge(parts):
    return stat([p[0] for p in parts], [1.0] * len(parts), [p[1] for p in parts])


def lse(blocks, axis):
    top = functools.reduce(
        jnp.maximum, [jnp.max(b, axis=axis, keepdims=True) for b in blocks]
    )
    total, mean = 0.0, 0.0
    for b in blocks:
        e = jnp.exp(b - top)
        total += jnp.sum(e, axis=axis, keepdims=True)
        mean += jnp.sum(e * b, axis=axis, keepdims=True)
    return top + jnp.log(total), mean / total


def own_kernel(s, a0, a1, b0, h, m, l, out, bh, bm, bl):
    n = a0.shape[0]
    for k, a in enumerate((a0, a1)):
        r = pl.ds(k * n, n)
        h[r], m[r], l[r] = three(a[...])
    put_three(b0[...], bh, bm, bl)
    out[...] = s[0] * scores(take((h, m, l)), take((bh, bm, bl)))


def near_kernel(s, h, m, l, b0, bp, bm, lp, lm, blocks_h, blocks_l, *parts):
    n = b0.shape[0]
    r = pl.ds(n, n)
    blocks_h[r], blocks_l[r] = two(b0[...])
    for k, (block, out) in enumerate(((bp, lp), (bm, lm))):
        put_three(block[...], *parts)
        r = pl.ds((k + 2) * n, n)
        blocks_h[r], blocks_l[r] = parts[0][...], parts[1][...]
        out[...] = s[0] * scores(take((h, m, l)), take(parts))


def near_stats_kernel(s, l0, lp, lm, top, mean, diag):
    n = l0.shape[1]
    t, m = lse([l0[...], lp[...], lm[...]], 1)
    top[...] = jnp.broadcast_to(t, top.shape)
    mean[...] = jnp.broadcast_to(m, mean.shape)
    i = lax.broadcasted_iota(jnp.int32, (n, n), 0)
    j = lax.broadcasted_iota(jnp.int32, (n, n), 1)
    diag[...] = jnp.sum(jnp.where(i == j, l0[0:n, :], 0.0), axis=0, keepdims=True)


def other_far(s, a, b, text):
    first = s[1] == 0.0
    return jnp.where(first, b[...], a[...]) if text else jnp.where(first, a[...], b[...])


def far_scores(s, parts, a, b, text, top, mean, lf, rows_out, blocks_h, blocks_l, *split):
    n = a.shape[0]
    for k, block in enumerate((a[...], other_far(s, a, b, text))):
        put_three(block, *split)
        r = pl.ds(4 * k * n, n)
        blocks_h[r], blocks_l[r] = split[0][...], split[1][...]
        r = pl.ds(k * n, n)
        lf[r, :] = s[0] * scores(take(parts, r), take(split))
    t, m = merge([(top[:, :1], mean[:, :1]), lse([lf[...]], 1)])
    rows_out[0:1, :] = row(t[:n])
    rows_out[1:2, :] = row(m[:n])
    rows_out[2:3, :] = row(t[n:])
    rows_out[3:4, :] = row(m[n:])


def text_far_kernel(s, xh, xm, xl, a, b, top, mean, old_h, old_l, lf, rows_out, *rest):
    far_scores(s, (xh, xm, xl), a, b, False, top, mean, lf, rows_out, *rest)


def image_far_kernel(s, yh, ym, yl, a, b, top, mean, old_h, old_l, image_rows, diag, lf, out, *rest):
    far_scores(s, (yh, ym, yl), a, b, True, top, mean, lf, out.at[4:8], *rest)
    out[0:4, :] = image_rows[...]
    out[8:9, :] = diag[...]
    out[9:16, :] = jnp.zeros((7, out.shape[1]), F32)


def merge_kernel(s, mine, got, out):
    pair = lambda ref, k: (ref[k : k + 1, :], ref[k + 1 : k + 2, :])
    n = out.shape[1]
    terms = []
    for k, ref, j in ((0, mine, 2), (2, got, 0)):
        row_stat = merge([pair(mine, k), pair(got, j)])
        col_stat = merge([pair(mine, k + 4), pair(got, j + 4)])
        out[k : k + 1, :] = row_stat[0]
        out[k + 1 : k + 2, :] = col_stat[0]
        diag = ref[8:9, :]
        terms.append(
            [
                jnp.sum(r + c - 2.0 * diag, axis=1, keepdims=True)
                for r, c in zip(row_stat, col_stat)
            ]
        )
    for k in range(2):
        both = terms[0][k] + terms[1][k]
        out[4 + k : 5 + k, :] = jnp.broadcast_to(both, (1, n))
    out[6:8, :] = jnp.zeros((2, n), F32)


def mate_kernel(s, own, m2, p2, out):
    out[...] = jnp.zeros_like(out)
    out[0:2, :] = own[4:6, :128] + jnp.where(s[2] == 0.0, p2[4:6, :128], m2[4:6, :128])


def sum_kernel(s, *refs):
    *terms, out = refs
    values = [t[...] for t in terms]
    while len(values) > 1:
        values = [a + b for a, b in zip(values[::2], values[1::2])]
    out[...] = values[0]


def last_kernel(s, a, b, loss, scale_grad):
    total = (a[...] + b[...]) * (1.0 / s[3])
    loss[...] = total[0:1, 0:1]
    scale_grad[...] = total[1:2, 0:1] / s[0]


def weigh(x, side, m):
    return jnp.exp(x - side) + jnp.exp(x - m)


def less_twice_eye(w):
    i = lax.broadcasted_iota(jnp.int32, w.shape, 0)
    j = lax.broadcasted_iota(jnp.int32, w.shape, 1)
    return jnp.where(i == j, w - 2.0, w)


def put_weights(text, sib, s, own, m2, p2, m4, p4, l0, lp, lm, lf, wh, wl):
    n = l0.shape[1]
    first = s[1] == 0.0
    rows = pl.ds(n if sib else 0, n)
    k = (2 if sib else 0) + (1 if text else 0)
    side = column(own[k : k + 1, :])
    other = slice(0, 1) if text else slice(1, 2)
    ahead, behind = p4[other, :], m4[other, :]
    if sib:
        far = jnp.where(first, ahead, behind)
    else:
        far = behind if text else ahead
    near = [(l0, own[other, :]), (lp, m2[other, :]), (lm, p2[other, :])]
    pieces = near + [(lf, far)] if sib else [(lf, far)] + near
    for k, (v, m) in enumerate(pieces):
        w = weigh(v[rows, :], side, m)
        if v is l0 and not sib:
            w = less_twice_eye(w)
        at = pl.ds(k * n, n)
        wh[:, at], wl[:, at] = two(w)


def tile_grads(wh, wl, bh, bl, rows, d):
    h, l = wh[...], wl[...]
    return (dot_nn(h, bl[rows, d]) + dot_nn(l, bh[rows, d])) + dot_nn(h, bh[rows, d])


def share_kernel(text, *refs):
    *args, bh, bl, out, wh, wl = refs
    put_weights(text, True, *args, wh, wl)
    n = out.shape[0]
    for k in range(out.shape[1] // TILE):
        d = pl.ds(k * TILE, TILE)
        out[:, d] = tile_grads(wh, wl, bh, bl, pl.ds(n, 4 * n), d)


def grads_kernel(text, *refs):
    *args, bh, bl, share, out, wh, wl, done, sem = refs
    put_weights(text, False, *args, wh, wl)
    n = share.shape[0]
    factor = 0.5 * args[0][0]
    copies = []
    for k in range(out.shape[1] // TILE):
        d = pl.ds(k * TILE, TILE)
        done[:, d] = factor * (
            tile_grads(wh, wl, bh, bl, pl.ds(0, 4 * n), d) + share[:, d]
        )
        copies.append(pltpu.make_async_copy(done.at[:, d], out.at[:, d], sem.at[k]))
        copies[-1].start()
    for copy in copies:
        copy.wait()


def on_device(image, text, scale):
    n, depth = image.shape
    device = lax.axis_index("dp")
    core, odd = (device % 2).astype(F32), (device // 2 % 2).astype(F32)
    s = jnp.stack([scale, core, odd, jnp.float32(2 * n * lax.axis_size("dp"))])
    block = ((n, depth), F32)
    both = ((2 * n, n), F32)
    part = ((2 * n, depth), BF16)
    wide = ((2 * n, 128), F32)
    four, line = ((4, n), F32), ((1, n), F32)
    split = [((n, depth), BF16)] * 3

    t_p, t_m = shift(text, 2), shift(text, -2)
    i_s, t_s = swap(image), swap(text)
    i_p, i_m = shift(image, 2), shift(image, -2)
    args = s, after(image, t_s), i_s, text
    *x, l0 = call(own_kernel, "text_own", 3.7, [part] * 3 + [both], args, split)
    args = s, after(text, l0), t_s, image
    *y, v0 = call(own_kernel, "image_own", 3.7, [part] * 3 + [both], args, split)
    t_p, t_m = after(t_p, v0), after(t_m, v0)
    t_pp, t_mm = shift(t_p, 2, (1,)), shift(t_m, -2)
    five = [((5 * n, depth), BF16)] * 2
    near_outs = [both] * 2 + five
    args = s, *x, text, t_p, t_m
    lp, lm, *t_parts = call(near_kernel, "text_near", 4.8, near_outs, args, split)
    args = s, l0, lp, lm
    top, mean, diag = call(near_stats_kernel, "text_stats", 1.8, [wide] * 2 + [line], args)
    i_p, i_m = after(i_p, top), after(i_m, top)
    i_pp, i_mm = shift(i_p, 2), shift(i_m, -2, (0,))
    args = s, *y, image, i_p, i_m
    vp, vm, *i_parts = call(near_kernel, "image_near", 4.8, near_outs, args, split)
    args = s, v0, vp, vm
    i_top, i_mean, _ = call(near_stats_kernel, "image_stats", 1.8, [wide] * 2 + [line], args)
    args = s, *x, after(t_mm, i_top), t_pp, top, mean, *t_parts
    outs = [both, four] + five
    kept = {8: 2, 9: 3}
    lf, image_rows, *t_parts = call(text_far_kernel, "text_far", 4.0, outs, args, split, alias=kept)
    args = s, *y, after(i_pp, lf), i_mm, i_top, i_mean, *i_parts, image_rows, diag
    outs = [both, ((16, n), F32)] + five
    vf, mine, *i_parts = call(image_far_kernel, "image_far", 4.0, outs, args, split, alias=kept)

    got = swap(mine)
    (own,) = call(merge_kernel, "merge", 0.6, [((8, n), F32)], (s, mine, got))
    m2, p2 = shift(own, 2), shift(own, -2)
    m4, p4 = shift(own, 4), shift(own, -4)
    terms = [((8, 128), F32)]
    (parts,) = call(mate_kernel, "pair", 0.5, terms, (s, own, m2, after(p2, m4, p4)))

    lses = m2, p2, m4, p4
    image_args = l0, lp, lm, lf, *t_parts
    text_args = v0, vp, vm, vf, *i_parts
    weights = [((n, 4 * n), BF16)] * 2
    final = weights + [block, pltpu.SemaphoreType.DMA((depth // TILE,))]
    kernel = functools.partial(share_kernel, False)
    args = s, own, *lses, *image_args
    (share,) = call(kernel, "image_share", 3.7, [block], args, weights)
    image_share = swap(share)
    y_parts = swap(parts, 16), swap(parts, 32), swap(parts, 48)
    args = s, after(parts, share), *y_parts
    (parts,) = call(sum_kernel, "sum_y", 0.5, terms, args)
    x_parts = swap(parts, 64), swap(parts, 128), swap(parts, 192)
    kernel = functools.partial(share_kernel, True)
    args = s, after(own, parts), *lses, *text_args
    (share,) = call(kernel, "text_share", 3.7, [block], args, weights)
    text_share = swap(share)
    args = s, after(parts, share), *x_parts
    (parts,) = call(sum_kernel, "sum_x", 0.5, terms, args)
    z_part = swap(parts, 4)
    kernel = functools.partial(grads_kernel, False)
    args = s, after(own, parts), *lses, *image_args, image_share
    (image_grad,) = call(kernel, "image_grads", 3.9, [block], args, final, ANY)
    args = s, after(parts, image_grad), z_part
    (parts,) = call(sum_kernel, "sum_z", 0.5, terms, args)
    z_part = swap(parts, 8)
    kernel = functools.partial(grads_kernel, True)
    args = s, after(own, parts), *lses, *text_args, text_share
    (text_grad,) = call(kernel, "text_grads", 3.9, [block], args, final, ANY)
    args = s, after(parts, text_grad), z_part
    loss, scale_grad = call(last_kernel, "last", 0.5, [((1, 1), F32)] * 2, args)
    return (loss.reshape(()), image_grad, text_grad, scale_grad.reshape(()))


def solution(mesh):
    in_specs = (P("dp", None), P("dp", None), P())
    out_specs = (P(), P("dp", None), P("dp", None), P())
    return jax.shard_map(
        on_device, mesh=mesh, in_specs=in_specs, out_specs=out_specs, check_vma=False
    )
```

```python
import functools

import jax
import jax.numpy as jnp
from jax import lax
from jax.experimental import pallas as pl
from jax.experimental.pallas import tpu as pltpu
from jax.sharding import PartitionSpec as P

WIN = 8
BOTH = (0, 1)
LIMIT = 10 * 1024 * 1024
TILE = 256
F32 = jnp.float32
BF16 = jnp.bfloat16
VMEM = pl.BlockSpec(memory_space=pltpu.VMEM)
SMEM = pl.BlockSpec(memory_space=pltpu.SMEM)
ANY = pl.BlockSpec(memory_space=pl.ANY)


def shift(value, steps, cores=BOTH):
    count = lax.axis_size("dp")
    pairs = [(s, (s + steps) % count) for s in range(count) if s % 2 in cores]
    return lax.ppermute(value, "dp", pairs)


def along(value, sign):
    count = lax.axis_size("dp")
    pairs = [(s, (s + sign * (2 + 2 * (s % 2))) % count) for s in range(count)]
    return lax.ppermute(value, "dp", pairs)


def swap(value, bit=1):
    count = lax.axis_size("dp")
    return lax.ppermute(value, "dp", [(s, s ^ bit) for s in range(count)])


def after(value, *done):
    return lax.optimization_barrier((value, done))[0]


def call(kernel, name, micros, outs, args, scratch=(), out_space=VMEM, alias=None):
    return pl.pallas_call(
        kernel,
        name=name,
        out_shape=[jax.ShapeDtypeStruct(s, d) for s, d in outs],
        in_specs=[SMEM] + [VMEM] * (len(args) - 1),
        out_specs=[out_space] * len(outs),
        scratch_shapes=[
            pltpu.VMEM(*x) if isinstance(x, tuple) else x for x in scratch
        ],
        compiler_params=pltpu.CompilerParams(vmem_limit_bytes=LIMIT),
        input_output_aliases=alias or {},
        cost_estimate=pl.CostEstimate(
            flops=int(micros * 1.15e9), bytes_accessed=1, transcendentals=0
        ),
    )(*args)


def dot_nt(a, b):
    return lax.dot_general(a, b, (((1,), (1,)), ((), ())), preferred_element_type=F32)


def dot_nn(a, b):
    return lax.dot_general(a, b, (((1,), (0,)), ((), ())), preferred_element_type=F32)


def two(x):
    h = x.astype(BF16)
    return h, (x - h.astype(F32)).astype(BF16)


def three(x):
    h = x.astype(BF16)
    r = x - h.astype(F32)
    m = r.astype(BF16)
    return h, m, (r - m.astype(F32)).astype(BF16)


def scores(a, b):
    (ah, am, al), (bh, bm, bl) = a, b
    small = dot_nt(ah, bl) + dot_nt(al, bh) + dot_nt(am, bm)
    return (small + (dot_nt(ah, bm) + dot_nt(am, bh))) + dot_nt(ah, bh)


def put_three(x, h, m, l):
    h[...], m[...], l[...] = three(x)


def take(refs, rows=slice(None)):
    return tuple(r[rows] for r in refs)


def column(v):
    return jnp.transpose(jnp.broadcast_to(v, (8, v.shape[1])))[:, :1]


def row(v):
    return jnp.transpose(jnp.broadcast_to(v, (v.shape[0], 128)))[:1]


def stat(tops, sums, means):
    top = functools.reduce(jnp.maximum, tops)
    total = sum(jnp.exp(t - top) * s for t, s in zip(tops, sums))
    mean = sum(jnp.exp(t - top) * m for t, m in zip(tops, means))
    return top + jnp.log(total), mean / total


def merge(parts):
    return stat([p[0] for p in parts], [1.0] * len(parts), [p[1] for p in parts])


def lse(blocks, axis):
    top = functools.reduce(
        jnp.maximum, [jnp.max(b, axis=axis, keepdims=True) for b in blocks]
    )
    total, mean = 0.0, 0.0
    for b in blocks:
        e = jnp.exp(b - top)
        total += jnp.sum(e, axis=axis, keepdims=True)
        mean += jnp.sum(e * b, axis=axis, keepdims=True)
    return top + jnp.log(total), mean / total


def own_kernel(s, a0, a1, b0, h, m, l, out, bh, bm, bl):
    n = a0.shape[0]
    for k, a in enumerate((a0, a1)):
        r = pl.ds(k * n, n)
        h[r], m[r], l[r] = three(a[...])
    put_three(b0[...], bh, bm, bl)
    out[...] = s[0] * scores(take((h, m, l)), take((bh, bm, bl)))


def near_kernel(s, h, m, l, b0, bm, bp, lp, lm, blocks_h, blocks_l, *parts):
    n = b0.shape[0]
    r = pl.ds(n, n)
    blocks_h[r], blocks_l[r] = two(b0[...])
    for k, (block, out) in enumerate(((bp, lp), (bm, lm))):
        put_three(block[...], *parts)
        r = pl.ds((k + 2) * n, n)
        blocks_h[r], blocks_l[r] = parts[0][...], parts[1][...]
        out[...] = s[0] * scores(take((h, m, l)), take(parts))


def near_stats_kernel(s, l0, lp, lm, top, mean, diag):
    n = l0.shape[1]
    t, m = lse([l0[...], lp[...], lm[...]], 1)
    top[...] = jnp.broadcast_to(t, top.shape)
    mean[...] = jnp.broadcast_to(m, mean.shape)
    i = lax.broadcasted_iota(jnp.int32, (n, n), 0)
    j = lax.broadcasted_iota(jnp.int32, (n, n), 1)
    diag[...] = jnp.sum(jnp.where(i == j, l0[0:n, :], 0.0), axis=0, keepdims=True)


def other_far(s, a, b, text):
    first = s[1] == 0.0
    return jnp.where(first, b[...], a[...]) if text else jnp.where(first, a[...], b[...])


def far_scores(s, parts, a, b, text, top, mean, lf, rows_out, blocks_h, blocks_l, *split):
    n = a.shape[0]
    for k, block in enumerate((a[...], other_far(s, a, b, text))):
        put_three(block, *split)
        r = pl.ds(4 * k * n, n)
        blocks_h[r], blocks_l[r] = split[0][...], split[1][...]
        r = pl.ds(k * n, n)
        lf[r, :] = s[0] * scores(take(parts, r), take(split))
    t, m = merge([(top[:, :1], mean[:, :1]), lse([lf[...]], 1)])
    rows_out[0:1, :] = row(t[:n])
    rows_out[1:2, :] = row(m[:n])
    rows_out[2:3, :] = row(t[n:])
    rows_out[3:4, :] = row(m[n:])


def text_far_kernel(s, xh, xm, xl, a, b, top, mean, old_h, old_l, lf, rows_out, *rest):
    far_scores(s, (xh, xm, xl), a, b, False, top, mean, lf, rows_out, *rest)


def image_far_kernel(s, yh, ym, yl, a, b, top, mean, old_h, old_l, image_rows, diag, lf, out, *rest):
    far_scores(s, (yh, ym, yl), a, b, True, top, mean, lf, out.at[4:8], *rest)
    out[0:4, :] = image_rows[...]
    out[8:9, :] = diag[...]
    out[9:16, :] = jnp.zeros((7, out.shape[1]), F32)


def merge_kernel(s, mine, got, out):
    pair = lambda ref, k: (ref[k : k + 1, :], ref[k + 1 : k + 2, :])
    n = out.shape[1]
    terms = []
    for k, ref, j in ((0, mine, 2), (2, got, 0)):
        row_stat = merge([pair(mine, k), pair(got, j)])
        col_stat = merge([pair(mine, k + 4), pair(got, j + 4)])
        out[k : k + 1, :] = row_stat[0]
        out[k + 1 : k + 2, :] = col_stat[0]
        diag = ref[8:9, :]
        terms.append(
            [
                jnp.sum(r + c - 2.0 * diag, axis=1, keepdims=True)
                for r, c in zip(row_stat, col_stat)
            ]
        )
    for k in range(2):
        both = terms[0][k] + terms[1][k]
        out[4 + k : 5 + k, :] = jnp.broadcast_to(both, (1, n))
    out[6:8, :] = jnp.zeros((2, n), F32)


def sort_kernel(s, own, v, vs, u, us, out, parts):
    first = s[1] == 0.0
    for k, (a, b) in enumerate(((u, us), (v, vs))):
        out[2 * k : 2 * k + 2, :] = jnp.where(first, a[0:2, :], b[2:4, :])
        out[2 * k + 4 : 2 * k + 6, :] = jnp.where(first, b[2:4, :], a[0:2, :])
    ahead = jnp.where(first, v[4:6, :128], vs[4:6, :128])
    behind = jnp.where(first, u[4:6, :128], us[4:6, :128])
    parts[...] = jnp.zeros_like(parts)
    parts[0:2, :] = own[4:6, :128] + jnp.where(s[2] == 0.0, ahead, behind)


def sum_kernel(s, a, b, out):
    out[...] = a[...] + b[...]


def last_kernel(s, a, b, loss, scale_grad):
    total = (a[...] + b[...]) * (1.0 / s[3])
    loss[...] = total[0:1, 0:1]
    scale_grad[...] = total[1:2, 0:1] / s[0]


def weigh(x, side, m):
    return jnp.exp(x - side) + jnp.exp(x - m)


def less_twice_eye(w):
    i = lax.broadcasted_iota(jnp.int32, w.shape, 0)
    j = lax.broadcasted_iota(jnp.int32, w.shape, 1)
    return jnp.where(i == j, w - 2.0, w)


def put_weights(text, sib, s, own, lses, l0, lp, lm, lf, wh, wl):
    n = l0.shape[1]
    first = s[1] == 0.0
    rows = pl.ds(n if sib else 0, n)
    k = (2 if sib else 0) + (1 if text else 0)
    side = column(own[k : k + 1, :])
    k = 0 if text else 1
    m2, p2, behind, ahead = (lses[j + k : j + k + 1, :] for j in (0, 2, 4, 6))
    if sib:
        far = jnp.where(first, ahead, behind)
    else:
        far = behind if text else ahead
    near = [(l0, own[k : k + 1, :]), (lp, m2), (lm, p2)]
    pieces = near + [(lf, far)] if sib else [(lf, far)] + near
    for k, (v, m) in enumerate(pieces):
        w = weigh(v[rows, :], side, m)
        if v is l0 and not sib:
            w = less_twice_eye(w)
        at = pl.ds(k * n, n)
        wh[:, at], wl[:, at] = two(w)


def tile_grads(wh, wl, bh, bl, rows, d):
    h, l = wh[...], wl[...]
    return (dot_nn(h, bl[rows, d]) + dot_nn(l, bh[rows, d])) + dot_nn(h, bh[rows, d])


def share_kernel(text, *refs):
    *args, bh, bl, out, wh, wl = refs
    put_weights(text, True, *args, wh, wl)
    n = out.shape[0]
    for k in range(out.shape[1] // TILE):
        d = pl.ds(k * TILE, TILE)
        out[:, d] = tile_grads(wh, wl, bh, bl, pl.ds(n, 4 * n), d)


def grads_kernel(text, *refs):
    *args, bh, bl, share, out, wh, wl, done, sem = refs
    put_weights(text, False, *args, wh, wl)
    n = share.shape[0]
    factor = 0.5 * args[0][0]
    copies = []
    for k in range(out.shape[1] // TILE):
        d = pl.ds(k * TILE, TILE)
        done[:, d] = factor * (
            tile_grads(wh, wl, bh, bl, pl.ds(0, 4 * n), d) + share[:, d]
        )
        copies.append(pltpu.make_async_copy(done.at[:, d], out.at[:, d], sem.at[k]))
        copies[-1].start()
    for copy in copies:
        copy.wait()


def on_device(image, text, scale):
    n, depth = image.shape
    device = lax.axis_index("dp")
    core, odd = (device % 2).astype(F32), (device // 2 % 2).astype(F32)
    s = jnp.stack([scale, core, odd, jnp.float32(2 * n * lax.axis_size("dp"))])
    block = ((n, depth), F32)
    both = ((2 * n, n), F32)
    part = ((2 * n, depth), BF16)
    wide = ((2 * n, 128), F32)
    four, line = ((4, n), F32), ((1, n), F32)
    split = [((n, depth), BF16)] * 3

    t_p, t_m = shift(text, 2), shift(text, -2)
    i_s, t_s = swap(image), swap(text)
    i_p, i_m = shift(image, 2), shift(image, -2)
    args = s, after(image, t_s), i_s, text
    *x, l0 = call(own_kernel, "text_own", 3.7, [part] * 3 + [both], args, split)
    args = s, after(text, l0), t_s, image
    *y, v0 = call(own_kernel, "image_own", 3.7, [part] * 3 + [both], args, split)
    t_p, t_m = after(t_p, v0), after(t_m, v0)
    t_pp, t_mm = shift(t_p, 2, (1,)), shift(t_m, -2)
    five = [((5 * n, depth), BF16)] * 2
    near_outs = [both] * 2 + five
    args = s, *x, text, t_m, t_p
    lp, lm, *t_parts = call(near_kernel, "text_near", 4.8, near_outs, args, split)
    args = s, l0, lp, lm
    top, mean, diag = call(near_stats_kernel, "text_stats", 1.8, [wide] * 2 + [line], args)
    i_p, i_m = after(i_p, top), after(i_m, top)
    i_pp, i_mm = shift(i_p, 2), shift(i_m, -2, (0,))
    args = s, *y, image, i_m, i_p
    vp, vm, *i_parts = call(near_kernel, "image_near", 4.8, near_outs, args, split)
    args = s, v0, vp, vm
    i_top, i_mean, _ = call(near_stats_kernel, "image_stats", 1.8, [wide] * 2 + [line], args)
    args = s, *x, after(t_mm, i_top), t_pp, top, mean, *t_parts
    outs = [both, four] + five
    kept = {8: 2, 9: 3}
    lf, image_rows, *t_parts = call(text_far_kernel, "text_far", 4.0, outs, args, split, alias=kept)
    args = s, *y, after(i_pp, lf), i_mm, i_top, i_mean, *i_parts, image_rows, diag
    outs = [both, ((16, n), F32)] + five
    vf, mine, *i_parts = call(image_far_kernel, "image_far", 4.0, outs, args, split, alias=kept)

    got = swap(mine)
    (own,) = call(merge_kernel, "merge", 0.6, [((8, n), F32)], (s, mine, got))
    u, v = along(own, 1), along(own, -1)
    args = s, own, v, swap(v), u, swap(u)
    terms = [((8, 128), F32)]
    lses, parts = call(sort_kernel, "sort", 0.5, [((8, n), F32)] + terms, args)

    def add(parts, bit, *done):
        args = s, after(parts, *done), swap(parts, bit)
        return call(sum_kernel, "sum", 0.5, terms, args)[0]

    image_args = l0, lp, lm, lf, *t_parts
    text_args = v0, vp, vm, vf, *i_parts
    weights = [((n, 4 * n), BF16)] * 2
    final = weights + [block, pltpu.SemaphoreType.DMA((depth // TILE,))]
    kernel = functools.partial(share_kernel, False)
    (share,) = call(kernel, "image_share", 3.1, [block], (s, own, lses, *image_args), weights)
    parts = add(parts, 16, share)
    image_share = swap(after(share, parts))
    kernel = functools.partial(share_kernel, True)
    args = s, after(own, parts), lses, *text_args
    (share,) = call(kernel, "text_share", 3.1, [block], args, weights)
    parts = add(parts, 32, share)
    text_share = swap(after(share, parts))
    parts = add(parts, 64)
    kernel = functools.partial(grads_kernel, False)
    args = s, after(own, parts), lses, *image_args, image_share
    (image_grad,) = call(kernel, "image_grads", 3.9, [block], args, final, ANY)
    parts = add(add(parts, 128, image_grad), 4)
    kernel = functools.partial(grads_kernel, True)
    args = s, after(own, parts), lses, *text_args, text_share
    (text_grad,) = call(kernel, "text_grads", 3.9, [block], args, final, ANY)
    z_part = swap(parts, 8)
    args = s, after(parts, text_grad), z_part
    loss, scale_grad = call(last_kernel, "last", 0.5, [((1, 1), F32)] * 2, args)
    return (loss.reshape(()), image_grad, text_grad, scale_grad.reshape(()))


def solution(mesh):
    in_specs = (P("dp", None), P("dp", None), P())
    out_specs = (P(), P("dp", None), P("dp", None), P())
    return jax.shard_map(
        on_device, mesh=mesh, in_specs=in_specs, out_specs=out_specs, check_vma=False
    )
```

```python
import functools

import jax
import jax.numpy as jnp
from jax import lax
from jax.experimental import pallas as pl
from jax.experimental.pallas import tpu as pltpu
from jax.sharding import PartitionSpec as P

WIN = 8
BOTH = (0, 1)
LIMIT = 10 * 1024 * 1024
TILE = 256
F32 = jnp.float32
BF16 = jnp.bfloat16
VMEM = pl.BlockSpec(memory_space=pltpu.VMEM)
SMEM = pl.BlockSpec(memory_space=pltpu.SMEM)
ANY = pl.BlockSpec(memory_space=pl.ANY)


def shift(value, steps, cores=BOTH):
    count = lax.axis_size("dp")
    pairs = [(s, (s + steps) % count) for s in range(count) if s % 2 in cores]
    return lax.ppermute(value, "dp", pairs)


def along(value, sign):
    count = lax.axis_size("dp")
    pairs = [(s, (s + sign * (2 + 2 * (s % 2))) % count) for s in range(count)]
    return lax.ppermute(value, "dp", pairs)


def swap(value, bit=1):
    count = lax.axis_size("dp")
    return lax.ppermute(value, "dp", [(s, s ^ bit) for s in range(count)])


def after(value, *done):
    return lax.optimization_barrier((value, done))[0]


def call(kernel, name, micros, outs, args, scratch=(), alias=None, in_hbm=(), out_hbm=()):
    return pl.pallas_call(
        kernel,
        name=name,
        out_shape=[jax.ShapeDtypeStruct(s, d) for s, d in outs],
        in_specs=[SMEM] + [ANY if k in in_hbm else VMEM for k in range(1, len(args))],
        out_specs=[ANY if k in out_hbm else VMEM for k in range(len(outs))],
        scratch_shapes=[pltpu.VMEM(*x) if isinstance(x, tuple) else x for x in scratch],
        compiler_params=pltpu.CompilerParams(vmem_limit_bytes=LIMIT),
        input_output_aliases=alias or {},
        cost_estimate=pl.CostEstimate(
            flops=int(micros * 1.15e9), bytes_accessed=1, transcendentals=0
        ),
    )(*args)


def dot_nt(a, b):
    return lax.dot_general(a, b, (((1,), (1,)), ((), ())), preferred_element_type=F32)


def dot_nn(a, b):
    return lax.dot_general(a, b, (((1,), (0,)), ((), ())), preferred_element_type=F32)


def two(x):
    h = x.astype(BF16)
    return h, (x - h.astype(F32)).astype(BF16)


def three(x):
    h = x.astype(BF16)
    r = x - h.astype(F32)
    m = r.astype(BF16)
    return h, m, (r - m.astype(F32)).astype(BF16)


def scores(a, b):
    (ah, am, al), (bh, bm, bl) = a, b
    small = dot_nt(ah, bl) + dot_nt(al, bh) + dot_nt(am, bm)
    return (small + (dot_nt(ah, bm) + dot_nt(am, bh))) + dot_nt(ah, bh)


def put_three(x, h, m, l):
    h[...], m[...], l[...] = three(x)


def take(refs, rows=slice(None)):
    return tuple(r[rows] for r in refs)


def column(v):
    return jnp.transpose(jnp.broadcast_to(v, (8, v.shape[1])))[:, :1]


def row(v):
    return jnp.transpose(jnp.broadcast_to(v, (v.shape[0], 128)))[:1]


def stat(tops, sums, means):
    top = functools.reduce(jnp.maximum, tops)
    total = sum(jnp.exp(t - top) * s for t, s in zip(tops, sums))
    mean = sum(jnp.exp(t - top) * m for t, m in zip(tops, means))
    return top + jnp.log(total), mean / total


def merge(parts):
    return stat([p[0] for p in parts], [1.0] * len(parts), [p[1] for p in parts])


def lse(blocks, axis):
    top = functools.reduce(
        jnp.maximum, [jnp.max(b, axis=axis, keepdims=True) for b in blocks]
    )
    total, mean = 0.0, 0.0
    for b in blocks:
        e = jnp.exp(b - top)
        total += jnp.sum(e, axis=axis, keepdims=True)
        mean += jnp.sum(e * b, axis=axis, keepdims=True)
    return top + jnp.log(total), mean / total


def own_kernel(s, a0, a1, b0, h, m, l, out, bh, bm, bl):
    n = a0.shape[0]
    for k, a in enumerate((a0, a1)):
        r = pl.ds(k * n, n)
        h[r], m[r], l[r] = three(a[...])
    put_three(b0[...], bh, bm, bl)
    out[...] = s[0] * scores(take((h, m, l)), take((bh, bm, bl)))


def near_kernel(s, h, m, l, b0, bm, bp, lp, lm, blocks_h, blocks_l, *parts):
    n = b0.shape[0]
    r = pl.ds(n, n)
    blocks_h[r], blocks_l[r] = two(b0[...])
    for k, (block, out) in enumerate(((bp, lp), (bm, lm))):
        put_three(block[...], *parts)
        r = pl.ds((k + 2) * n, n)
        blocks_h[r], blocks_l[r] = parts[0][...], parts[1][...]
        out[...] = s[0] * scores(take((h, m, l)), take(parts))


def near_stats_kernel(s, l0, lp, lm, top, mean, diag):
    n = l0.shape[1]
    t, m = lse([l0[...], lp[...], lm[...]], 1)
    top[...] = jnp.broadcast_to(t, top.shape)
    mean[...] = jnp.broadcast_to(m, mean.shape)
    i = lax.broadcasted_iota(jnp.int32, (n, n), 0)
    j = lax.broadcasted_iota(jnp.int32, (n, n), 1)
    diag[...] = jnp.sum(jnp.where(i == j, l0[0:n, :], 0.0), axis=0, keepdims=True)


def put_far(s, parts, k, block, lf, blocks_h, blocks_l, split):
    n = block.shape[0]
    put_three(block, *split)
    r = pl.ds(4 * k * n, n)
    blocks_h[r], blocks_l[r] = split[0][...], split[1][...]
    r = pl.ds(k * n, n)
    lf[r, :] = s[0] * scores(take(parts, r), take(split))


def put_rows(k, top, mean, lf, out, at):
    n = lf.shape[1]
    r = pl.ds(k * n, n)
    t, m = merge([(top[r, :1], mean[r, :1]), lse([lf[r, :]], 1)])
    out[at : at + 1, :] = row(t)
    out[at + 1 : at + 2, :] = row(m)


def text_far_kernel(s, xh, xm, xl, a, b, top, mean, old_h, old_l, lf, rows_out, blocks_h, blocks_l, *split):
    first = s[1] == 0.0
    for k, block in ((0, a[...]), (1, jnp.where(first, a[...], b[...]))):
        put_far(s, (xh, xm, xl), k, block, lf, blocks_h, blocks_l, split)
        put_rows(k, top, mean, lf, rows_out, 2 * k)


def image_behind_kernel(s, yh, ym, yl, block, top, mean, old_h, old_l, image_rows, diag, lf, out, blocks_h, blocks_l, *split):
    n = block.shape[0]
    put_far(s, (yh, ym, yl), 0, block[...], lf, blocks_h, blocks_l, split)
    put_rows(0, top, mean, lf, out, 4)
    out[0:4, :] = image_rows[...]
    out[8:9, :] = diag[...]
    out[9:16, :] = jnp.zeros((7, n), F32)

    @pl.when(s[1] != 0.0)
    def _():
        put_far(s, (yh, ym, yl), 1, block[...], lf, blocks_h, blocks_l, split)
        put_rows(1, top, mean, lf, out, 6)


def image_ahead_kernel(s, yh, ym, yl, block, top, mean, old_h, old_l, old_lf, old, lf, out, blocks_h, blocks_l, *split):
    @pl.when(s[1] == 0.0)
    def _():
        put_far(s, (yh, ym, yl), 1, block[...], lf, blocks_h, blocks_l, split)
        put_rows(1, top, mean, lf, out, 6)


def merge_kernel(s, mine, got, out):
    pair = lambda ref, k: (ref[k : k + 1, :], ref[k + 1 : k + 2, :])
    n = out.shape[1]
    terms = []
    for k, ref, j in ((0, mine, 2), (2, got, 0)):
        row_stat = merge([pair(mine, k), pair(got, j)])
        col_stat = merge([pair(mine, k + 4), pair(got, j + 4)])
        out[k : k + 1, :] = row_stat[0]
        out[k + 1 : k + 2, :] = col_stat[0]
        diag = ref[8:9, :]
        terms.append(
            [
                jnp.sum(r + c - 2.0 * diag, axis=1, keepdims=True)
                for r, c in zip(row_stat, col_stat)
            ]
        )
    for k in range(2):
        both = terms[0][k] + terms[1][k]
        out[4 + k : 5 + k, :] = jnp.broadcast_to(both, (1, n))
    out[6:8, :] = jnp.zeros((2, n), F32)


def sort_kernel(s, own, v, vs, u, us, out):
    first = s[1] == 0.0
    for k, (a, b) in enumerate(((u, us), (v, vs))):
        out[2 * k : 2 * k + 2, :] = jnp.where(first, a[0:2, :], b[2:4, :])
        out[2 * k + 4 : 2 * k + 6, :] = jnp.where(first, b[2:4, :], a[0:2, :])


def pair_kernel(s, own, mate, out):
    out[...] = jnp.zeros_like(out)
    out[0:2, :] = own[4:6, :128] + mate[4:6, :128]


def paired(values):
    if len(values) == 1:
        return values[0]
    return paired([a + b for a, b in zip(values[::2], values[1::2])])


def sum_kernel(s, *refs):
    refs[-1][...] = paired([r[...] for r in refs[:-1]])


def last_kernel(s, *refs):
    *terms, loss, scale_grad = refs
    total = paired([t[...] for t in terms]) * (1.0 / s[2])
    loss[...] = total[0:1, 0:1]
    scale_grad[...] = total[1:2, 0:1] / s[0]


def weigh(x, side, m):
    return jnp.exp(x - side) + jnp.exp(x - m)


def less_twice_eye(w):
    i = lax.broadcasted_iota(jnp.int32, w.shape, 0)
    j = lax.broadcasted_iota(jnp.int32, w.shape, 1)
    return jnp.where(i == j, w - 2.0, w)


def put_weights(text, sib, s, own, lses, l0, lp, lm, lf, wh, wl):
    n = l0.shape[1]
    first = s[1] == 0.0
    rows = pl.ds(n if sib else 0, n)
    k = (2 if sib else 0) + (1 if text else 0)
    side = column(own[k : k + 1, :])
    k = 0 if text else 1
    m2, p2, behind, ahead = (lses[j + k : j + k + 1, :] for j in (0, 2, 4, 6))
    if sib:
        far = jnp.where(first, ahead, behind)
    else:
        far = behind if text else ahead
    near = [(l0, own[k : k + 1, :]), (lp, m2), (lm, p2)]
    pieces = near + [(lf, far)] if sib else [(lf, far)] + near
    for k, (v, m) in enumerate(pieces):
        w = weigh(v[rows, :], side, m)
        if v is l0 and not sib:
            w = less_twice_eye(w)
        at = pl.ds(k * n, n)
        wh[:, at], wl[:, at] = two(w)


def tile_grads(wh, wl, bh, bl, rows, d):
    h, l = wh[...], wl[...]
    return (dot_nn(h, bl[rows, d]) + dot_nn(l, bh[rows, d])) + dot_nn(h, bh[rows, d])


def share_kernel(text, *refs):
    *args, bh, bl, out, wh, wl = refs
    put_weights(text, True, *args, wh, wl)
    n = out.shape[0]
    for k in range(out.shape[1] // TILE):
        d = pl.ds(k * TILE, TILE)
        out[:, d] = tile_grads(wh, wl, bh, bl, pl.ds(n, 4 * n), d)


def grads_kernel(text, *refs):
    *args, bh, bl, share, out, wh, wl, done, sem = refs
    put_weights(text, False, *args, wh, wl)
    n = share.shape[0]
    factor = 0.5 * args[0][0]
    copies = []
    for k in range(out.shape[1] // TILE):
        d = pl.ds(k * TILE, TILE)
        total = tile_grads(wh, wl, bh, bl, pl.ds(0, 4 * n), d) + share[:, d]
        done[:, d] = factor * total
        copies.append(pltpu.make_async_copy(done.at[:, d], out.at[:, d], sem.at[k]))
        copies[-1].start()
    for copy in copies:
        copy.wait()


def on_device(image, text, scale):
    n, depth = image.shape
    device = lax.axis_index("dp")
    core = (device % 2).astype(F32)
    s = jnp.stack([scale, core, jnp.float32(2 * n * lax.axis_size("dp"))])
    block = ((n, depth), F32)
    both = ((2 * n, n), F32)
    part = ((2 * n, depth), BF16)
    wide = ((2 * n, 128), F32)
    four, line = ((4, n), F32), ((1, n), F32)
    split = [((n, depth), BF16)] * 3

    t_p, t_m = shift(text, 2), shift(text, -2)
    i_s, t_s = swap(image), swap(text)
    i_p, i_m = shift(image, 2), shift(image, -2)
    args = s, after(image, t_s), i_s, text
    *x, l0 = call(own_kernel, "text_own", 3.7, [part] * 3 + [both], args, split)
    args = s, after(text, l0), t_s, image
    *y, v0 = call(own_kernel, "image_own", 3.7, [part] * 3 + [both], args, split)
    t_p, t_m = after(t_p, v0), after(t_m, v0)
    t_pp, t_mm = shift(t_p, 2, (1,)), shift(t_m, -2)
    five = [((5 * n, depth), BF16)] * 2
    near_outs = [both] * 2 + five
    args = s, *x, text, t_m, t_p
    lp, lm, *t_parts = call(near_kernel, "text_near", 4.8, near_outs, args, split)
    args = s, l0, lp, lm
    top, mean, diag = call(near_stats_kernel, "text_stats", 1.8, [wide] * 2 + [line], args)
    i_p, i_m = after(i_p, top), after(i_m, top)
    i_pp, i_mm = shift(i_p, 2), shift(i_m, -2, (0,))
    args = s, *y, image, i_m, i_p
    vp, vm, *i_parts = call(near_kernel, "image_near", 4.8, near_outs, args, split)
    args = s, v0, vp, vm
    i_top, i_mean, _ = call(near_stats_kernel, "image_stats", 1.8, [wide] * 2 + [line], args)
    args = s, *x, after(t_mm, i_top), t_pp, top, mean, *t_parts
    outs = [both, four] + five
    kept = {8: 2, 9: 3}
    lf, image_rows, *t_parts = call(text_far_kernel, "text_far", 4.0, outs, args, split, kept)
    args = s, *y, after(i_pp, lf), i_top, i_mean, *i_parts, image_rows, diag
    outs = [both, ((16, n), F32)] + five
    kept = {7: 2, 8: 3}
    vf, mine, *i_parts = call(image_behind_kernel, "image_behind", 3.0, outs, args, split, kept)
    args = s, *y, i_mm, i_top, i_mean, *i_parts, vf, mine
    kept = {7: 2, 8: 3, 9: 0, 10: 1}
    vf, mine, *i_parts = call(image_ahead_kernel, "image_ahead", 2.0, outs, args, split, kept)

    got = swap(mine)
    (own,) = call(merge_kernel, "merge", 0.6, [((8, n), F32)], (s, mine, got))
    u, v = along(own, 1), along(own, -1)
    terms = [((8, 128), F32)]
    (parts,) = call(pair_kernel, "pair", 0.5, terms, (s, own, swap(own, 2)))

    def add(parts, bits, *done):
        args = s, after(parts, *done), *(swap(parts, b) for b in bits)
        return call(sum_kernel, "sum", 0.5, terms, args)[0]

    parts = add(parts, (4,))
    args = s, after(own, parts), v, swap(v), u, swap(u)
    (lses,) = call(sort_kernel, "sort", 0.5, [((8, n), F32)], args)

    image_args = l0, lp, lm, lf, *t_parts
    text_args = v0, vp, vm, vf, *i_parts
    weights = [((n, 4 * n), BF16)] * 2
    final = [block, pltpu.SemaphoreType.DMA((depth // TILE,))]
    kernel = functools.partial(share_kernel, False)
    (share,) = call(kernel, "image_share", 3.1, [block], (s, own, lses, *image_args), weights)
    parts = add(parts, (8,), share)
    image_share = swap(after(share, parts))
    kernel = functools.partial(share_kernel, True)
    args = s, after(own, parts), lses, *text_args
    (share,) = call(kernel, "text_share", 3.1, [block], args, weights)
    parts = add(parts, (64, 128, 192), share)
    text_share = swap(after(share, parts))

    y_part = swap(parts, 32)
    kernel = functools.partial(grads_kernel, False)
    args = s, after(own, parts), lses, *image_args, image_share
    final = weights + final
    (image_grad,) = call(kernel, "image_grads", 3.9, [block], args, final, out_hbm=(0,))
    args = s, after(parts, image_grad), y_part
    (parts,) = call(sum_kernel, "sum", 0.5, terms, args)
    y_part = swap(parts, 16)
    kernel = functools.partial(grads_kernel, True)
    args = s, after(own, parts), lses, *text_args, text_share
    (text_grad,) = call(kernel, "text_grads", 3.9, [block], args, final, out_hbm=(0,))
    args = s, after(parts, text_grad), y_part
    loss, scale_grad = call(last_kernel, "last", 0.5, [((1, 1), F32)] * 2, args)
    return (loss.reshape(()), image_grad, text_grad, scale_grad.reshape(()))


def solution(mesh):
    in_specs = (P("dp", None), P("dp", None), P())
    out_specs = (P(), P("dp", None), P("dp", None), P())
    return jax.shard_map(
        on_device, mesh=mesh, in_specs=in_specs, out_specs=out_specs, check_vma=False
    )
```

```python
import functools

import jax
import jax.numpy as jnp
from jax import lax
from jax.experimental import pallas as pl
from jax.experimental.pallas import tpu as pltpu
from jax.sharding import PartitionSpec as P

WIN = 8
BOTH = (0, 1)
LIMIT = 10 * 1024 * 1024
TILE = 256
F32 = jnp.float32
BF16 = jnp.bfloat16
VMEM = pl.BlockSpec(memory_space=pltpu.VMEM)
SMEM = pl.BlockSpec(memory_space=pltpu.SMEM)
ANY = pl.BlockSpec(memory_space=pl.ANY)


def shift(value, steps, cores=BOTH):
    count = lax.axis_size("dp")
    pairs = [(s, (s + steps) % count) for s in range(count) if s % 2 in cores]
    return lax.ppermute(value, "dp", pairs)


def along(value, sign):
    count = lax.axis_size("dp")
    pairs = [(s, (s + sign * (2 + 2 * (s % 2))) % count) for s in range(count)]
    return lax.ppermute(value, "dp", pairs)


def swap(value, bit=1):
    count = lax.axis_size("dp")
    return lax.ppermute(value, "dp", [(s, s ^ bit) for s in range(count)])


def after(value, *done):
    return lax.optimization_barrier((value, done))[0]


def call(kernel, name, micros, outs, args, scratch=(), alias=None, in_hbm=(), out_hbm=()):
    return pl.pallas_call(
        kernel,
        name=name,
        out_shape=[jax.ShapeDtypeStruct(s, d) for s, d in outs],
        in_specs=[SMEM] + [ANY if k in in_hbm else VMEM for k in range(1, len(args))],
        out_specs=[ANY if k in out_hbm else VMEM for k in range(len(outs))],
        scratch_shapes=[pltpu.VMEM(*x) if isinstance(x, tuple) else x for x in scratch],
        compiler_params=pltpu.CompilerParams(vmem_limit_bytes=LIMIT),
        input_output_aliases=alias or {},
        cost_estimate=pl.CostEstimate(
            flops=int(micros * 1.15e9), bytes_accessed=1, transcendentals=0
        ),
    )(*args)


def dot_nt(a, b):
    return lax.dot_general(a, b, (((1,), (1,)), ((), ())), preferred_element_type=F32)


def dot_nn(a, b):
    return lax.dot_general(a, b, (((1,), (0,)), ((), ())), preferred_element_type=F32)


def two(x):
    h = x.astype(BF16)
    return h, (x - h.astype(F32)).astype(BF16)


def three(x):
    h = x.astype(BF16)
    r = x - h.astype(F32)
    m = r.astype(BF16)
    return h, m, (r - m.astype(F32)).astype(BF16)


def scores(a, b):
    (ah, am, al), (bh, bm, bl) = a, b
    small = dot_nt(ah, bl) + dot_nt(al, bh) + dot_nt(am, bm)
    return (small + (dot_nt(ah, bm) + dot_nt(am, bh))) + dot_nt(ah, bh)


def put_three(x, h, m, l):
    h[...], m[...], l[...] = three(x)


def take(refs, rows=slice(None)):
    return tuple(r[rows] for r in refs)


def column(v):
    return jnp.transpose(jnp.broadcast_to(v, (8, v.shape[1])))[:, :1]


def row(v):
    return jnp.transpose(jnp.broadcast_to(v, (v.shape[0], 128)))[:1]


def stat(tops, sums, means):
    top = functools.reduce(jnp.maximum, tops)
    total = sum(jnp.exp(t - top) * s for t, s in zip(tops, sums))
    mean = sum(jnp.exp(t - top) * m for t, m in zip(tops, means))
    return top + jnp.log(total), mean / total


def merge(parts):
    return stat([p[0] for p in parts], [1.0] * len(parts), [p[1] for p in parts])


def lse(blocks, axis):
    top = functools.reduce(
        jnp.maximum, [jnp.max(b, axis=axis, keepdims=True) for b in blocks]
    )
    total, mean = 0.0, 0.0
    for b in blocks:
        e = jnp.exp(b - top)
        total += jnp.sum(e, axis=axis, keepdims=True)
        mean += jnp.sum(e * b, axis=axis, keepdims=True)
    return top + jnp.log(total), mean / total


def own_kernel(s, a0, a1, b0, h, m, l, out, bh, bm, bl):
    n = a0.shape[0]
    for k, a in enumerate((a0, a1)):
        r = pl.ds(k * n, n)
        h[r], m[r], l[r] = three(a[...])
    put_three(b0[...], bh, bm, bl)
    out[...] = s[0] * scores(take((h, m, l)), take((bh, bm, bl)))


def near_kernel(s, h, m, l, b0, bm, bp, lp, lm, blocks_h, blocks_l, *parts):
    n = b0.shape[0]
    r = pl.ds(0, n)
    blocks_h[r], blocks_l[r] = two(b0[...])
    for k, (block, out) in enumerate(((bp, lp), (bm, lm))):
        put_three(block[...], *parts)
        r = pl.ds((k + 2) * n, n)
        blocks_h[r], blocks_l[r] = parts[0][...], parts[1][...]
        out[...] = s[0] * scores(take((h, m, l)), take(parts))


def near_stats_kernel(s, l0, lp, lm, top, mean, diag):
    n = l0.shape[1]
    t, m = lse([l0[...], lp[...], lm[...]], 1)
    top[...] = jnp.broadcast_to(t, top.shape)
    mean[...] = jnp.broadcast_to(m, mean.shape)
    i = lax.broadcasted_iota(jnp.int32, (n, n), 0)
    j = lax.broadcasted_iota(jnp.int32, (n, n), 1)
    diag[...] = jnp.sum(jnp.where(i == j, l0[0:n, :], 0.0), axis=0, keepdims=True)


def put_far(s, parts, k, block, lf, blocks_h, blocks_l, split):
    n = block.shape[0]
    put_three(block, *split)
    r = pl.ds((1 + 3 * k) * n, n)
    blocks_h[r], blocks_l[r] = split[0][...], split[1][...]
    r = pl.ds(k * n, n)
    lf[r, :] = s[0] * scores(take(parts, r), take(split))


def put_rows(k, top, mean, lf, out, at):
    n = lf.shape[1]
    r = pl.ds(k * n, n)
    t, m = merge([(top[r, :1], mean[r, :1]), lse([lf[r, :]], 1)])
    out[at : at + 1, :] = row(t)
    out[at + 1 : at + 2, :] = row(m)


def text_far_kernel(s, xh, xm, xl, a, b, top, mean, old_h, old_l, lf, rows_out, blocks_h, blocks_l, *split):
    first = s[1] == 0.0
    for k, block in ((0, a[...]), (1, jnp.where(first, a[...], b[...]))):
        put_far(s, (xh, xm, xl), k, block, lf, blocks_h, blocks_l, split)
        put_rows(k, top, mean, lf, rows_out, 2 * k)


def image_behind_kernel(s, yh, ym, yl, block, top, mean, old_h, old_l, image_rows, diag, lf, out, blocks_h, blocks_l, *split):
    n = block.shape[0]
    put_far(s, (yh, ym, yl), 0, block[...], lf, blocks_h, blocks_l, split)
    put_rows(0, top, mean, lf, out, 4)
    out[0:4, :] = image_rows[...]
    out[8:9, :] = diag[...]
    out[9:16, :] = jnp.zeros((7, n), F32)

    @pl.when(s[1] != 0.0)
    def _():
        put_far(s, (yh, ym, yl), 1, block[...], lf, blocks_h, blocks_l, split)
        put_rows(1, top, mean, lf, out, 6)


def image_ahead_kernel(s, yh, ym, yl, block, top, mean, old_h, old_l, old_lf, old, lf, out, blocks_h, blocks_l, *split):
    @pl.when(s[1] == 0.0)
    def _():
        put_far(s, (yh, ym, yl), 1, block[...], lf, blocks_h, blocks_l, split)
        put_rows(1, top, mean, lf, out, 6)


def merge_kernel(s, mine, got, out):
    pair = lambda ref, k: (ref[k : k + 1, :], ref[k + 1 : k + 2, :])
    n = out.shape[1]
    terms = []
    for k, ref, j in ((0, mine, 2), (2, got, 0)):
        row_stat = merge([pair(mine, k), pair(got, j)])
        col_stat = merge([pair(mine, k + 4), pair(got, j + 4)])
        out[k : k + 1, :] = row_stat[0]
        out[k + 1 : k + 2, :] = col_stat[0]
        diag = ref[8:9, :]
        terms.append(
            [
                jnp.sum(r + c - 2.0 * diag, axis=1, keepdims=True)
                for r, c in zip(row_stat, col_stat)
            ]
        )
    for k in range(2):
        both = terms[0][k] + terms[1][k]
        out[4 + k : 5 + k, :] = jnp.broadcast_to(both, (1, n))
    out[6:8, :] = jnp.zeros((2, n), F32)


def sort_kernel(s, own, v, vs, u, us, out):
    first = s[1] == 0.0
    for k, (a, b) in enumerate(((u, us), (v, vs))):
        out[2 * k : 2 * k + 2, :] = jnp.where(first, a[0:2, :], b[2:4, :])
        out[2 * k + 4 : 2 * k + 6, :] = jnp.where(first, b[2:4, :], a[0:2, :])


def pair_kernel(s, own, mate, out):
    out[...] = jnp.zeros_like(out)
    out[0:2, :] = own[4:6, :128] + mate[4:6, :128]


def paired(values):
    if len(values) == 1:
        return values[0]
    return paired([a + b for a, b in zip(values[::2], values[1::2])])


def sum_kernel(s, *refs):
    refs[-1][...] = paired([r[...] for r in refs[:-1]])


def last_kernel(s, *refs):
    *terms, loss, scale_grad = refs
    total = paired([t[...] for t in terms]) * (1.0 / s[2])
    loss[...] = total[0:1, 0:1]
    scale_grad[...] = total[1:2, 0:1] / s[0]


def weigh(x, side, m):
    return jnp.exp(x - side) + jnp.exp(x - m)


def less_twice_eye(w):
    i = lax.broadcasted_iota(jnp.int32, w.shape, 0)
    j = lax.broadcasted_iota(jnp.int32, w.shape, 1)
    return jnp.where(i == j, w - 2.0, w)


def put_weights(text, sib, s, own, lses, lp, lm, lf, wh, wl):
    n = lp.shape[1]
    first = s[1] == 0.0
    rows = pl.ds(n if sib else 0, n)
    k = (2 if sib else 0) + (1 if text else 0)
    side = column(own[k : k + 1, :])
    k = 0 if text else 1
    m2, p2, behind, ahead = (lses[j + k : j + k + 1, :] for j in (0, 2, 4, 6))
    if sib:
        far = jnp.where(first, ahead, behind)
    else:
        far = behind if text else ahead
    near = [(lp, m2), (lm, p2)]
    pieces = near + [(lf, far)] if sib else [(lf, far)] + near
    for k, (v, m) in enumerate(pieces):
        w = weigh(v[rows, :], side, m)
        at = pl.ds(k * n, n)
        wh[:, at], wl[:, at] = two(w)


def tile_grads(wh, wl, bh, bl, rows, d):
    h, l = wh[...], wl[...]
    return (dot_nn(h, bl[rows, d]) + dot_nn(l, bh[rows, d])) + dot_nn(h, bh[rows, d])


def own_blocks_kernel(s, own, l0, v0, th, tl, ih, il, image_out, text_out, wh, wl):
    n = l0.shape[1]
    for text, x, bh, bl, out in ((0, l0, th, tl, image_out), (1, v0, ih, il, text_out)):
        side = jnp.concatenate(
            [column(own[text : text + 1, :]), column(own[text + 2 : text + 3, :])]
        )
        w = weigh(x[...], side, own[1 - text : 2 - text, :])
        wh[...], wl[...] = two(less_twice_eye(w))
        for k in range(out.shape[1] // TILE):
            d = pl.ds(k * TILE, TILE)
            out[:, d] = tile_grads(wh, wl, bh, bl, pl.ds(0, n), d)


def share_kernel(text, *refs):
    *args, bh, bl, first, out, wh, wl = refs
    put_weights(text, True, *args, wh, wl)
    n = out.shape[0]
    for k in range(out.shape[1] // TILE):
        d = pl.ds(k * TILE, TILE)
        total = tile_grads(wh, wl, bh, bl, pl.ds(2 * n, 3 * n), d)
        out[:, d] = total + first[n:, d]


def grads_kernel(text, *refs):
    *args, bh, bl, first, share, out, wh, wl, done, sem = refs
    put_weights(text, False, *args, wh, wl)
    n = share.shape[0]
    factor = 0.5 * args[0][0]
    copies = []
    for k in range(out.shape[1] // TILE):
        d = pl.ds(k * TILE, TILE)
        total = tile_grads(wh, wl, bh, bl, pl.ds(n, 3 * n), d)
        done[:, d] = factor * ((total + first[0:n, d]) + share[:, d])
        copies.append(pltpu.make_async_copy(done.at[:, d], out.at[:, d], sem.at[k]))
        copies[-1].start()
    for copy in copies:
        copy.wait()


def on_device(image, text, scale):
    n, depth = image.shape
    device = lax.axis_index("dp")
    core = (device % 2).astype(F32)
    s = jnp.stack([scale, core, jnp.float32(2 * n * lax.axis_size("dp"))])
    block = ((n, depth), F32)
    both = ((2 * n, n), F32)
    part = ((2 * n, depth), BF16)
    wide = ((2 * n, 128), F32)
    four, line = ((4, n), F32), ((1, n), F32)
    split = [((n, depth), BF16)] * 3

    t_p, t_m = shift(text, 2), shift(text, -2)
    i_s, t_s = swap(image), swap(text)
    i_p, i_m = shift(image, 2), shift(image, -2)
    args = s, after(image, t_s), i_s, text
    *x, l0 = call(own_kernel, "text_own", 3.7, [part] * 3 + [both], args, split)
    args = s, after(text, l0), t_s, image
    *y, v0 = call(own_kernel, "image_own", 3.7, [part] * 3 + [both], args, split)
    t_p, t_m = after(t_p, v0), after(t_m, v0)
    t_pp, t_mm = shift(t_p, 2, (1,)), shift(t_m, -2)
    five = [((5 * n, depth), BF16)] * 2
    near_outs = [both] * 2 + five
    args = s, *x, text, t_m, t_p
    lp, lm, *t_parts = call(near_kernel, "text_near", 4.8, near_outs, args, split)
    args = s, l0, lp, lm
    top, mean, diag = call(near_stats_kernel, "text_stats", 1.8, [wide] * 2 + [line], args)
    i_p, i_m = after(i_p, top), after(i_m, top)
    i_pp, i_mm = shift(i_p, 2), shift(i_m, -2, (0,))
    args = s, *y, image, i_m, i_p
    vp, vm, *i_parts = call(near_kernel, "image_near", 4.8, near_outs, args, split)
    args = s, v0, vp, vm
    i_top, i_mean, _ = call(near_stats_kernel, "image_stats", 1.8, [wide] * 2 + [line], args)
    args = s, *x, after(t_mm, i_top), t_pp, top, mean, *t_parts
    outs = [both, four] + five
    kept = {8: 2, 9: 3}
    lf, image_rows, *t_parts = call(text_far_kernel, "text_far", 4.0, outs, args, split, kept)
    args = s, *y, after(i_pp, lf), i_top, i_mean, *i_parts, image_rows, diag
    outs = [both, ((16, n), F32)] + five
    kept = {7: 2, 8: 3}
    vf, mine, *i_parts = call(image_behind_kernel, "image_behind", 3.0, outs, args, split, kept)
    args = s, *y, i_mm, i_top, i_mean, *i_parts, vf, mine
    kept = {7: 2, 8: 3, 9: 0, 10: 1}
    vf, mine, *i_parts = call(image_ahead_kernel, "image_ahead", 2.0, outs, args, split, kept)

    got = swap(mine)
    (own,) = call(merge_kernel, "merge", 0.6, [((8, n), F32)], (s, mine, got))
    u, v = along(own, 1), along(own, -1)
    terms = [((8, 128), F32)]
    (parts,) = call(pair_kernel, "pair", 0.5, terms, (s, own, swap(own, 2)))

    def add(parts, bits, *done):
        args = s, after(parts, *done), *(swap(parts, b) for b in bits)
        return call(sum_kernel, "sum", 0.5, terms, args)[0]

    parts = add(parts, (4,))
    args = s, own, l0, v0, *t_parts, *i_parts
    firsts = [((2 * n, depth), F32)] * 2
    w_part = [((2 * n, n), BF16)] * 2
    image_first, text_first = call(own_blocks_kernel, "own_blocks", 3.0, firsts, args, w_part)
    args = s, after(own, parts), v, swap(after(v, image_first)), u, swap(u)
    (lses,) = call(sort_kernel, "sort", 0.5, [((8, n), F32)], args)

    image_args = lp, lm, lf, *t_parts, image_first
    text_args = vp, vm, vf, *i_parts, text_first
    weights = [((n, 3 * n), BF16)] * 2
    final = [block, pltpu.SemaphoreType.DMA((depth // TILE,))]
    kernel = functools.partial(share_kernel, False)
    (share,) = call(kernel, "image_share", 3.1, [block], (s, own, lses, *image_args), weights)
    parts = add(parts, (16,), share)
    image_share = swap(after(share, parts))
    kernel = functools.partial(share_kernel, True)
    args = s, after(own, parts), lses, *text_args
    (share,) = call(kernel, "text_share", 3.1, [block], args, weights)
    parts = add(parts, (64, 128, 192), share)
    text_share = swap(after(share, parts))

    far_part = swap(parts, 8)
    kernel = functools.partial(grads_kernel, False)
    args = s, after(own, parts), lses, *image_args, image_share
    final = weights + final
    (image_grad,) = call(kernel, "image_grads", 3.9, [block], args, final, out_hbm=(0,))
    args = s, after(parts, image_grad), far_part
    (parts,) = call(sum_kernel, "sum", 0.5, terms, args)
    y_part = swap(parts, 32)
    kernel = functools.partial(grads_kernel, True)
    args = s, after(own, parts), lses, *text_args, text_share
    (text_grad,) = call(kernel, "text_grads", 3.9, [block], args, final, out_hbm=(0,))
    args = s, after(parts, text_grad), y_part
    loss, scale_grad = call(last_kernel, "last", 0.5, [((1, 1), F32)] * 2, args)
    return (loss.reshape(()), image_grad, text_grad, scale_grad.reshape(()))


def solution(mesh):
    in_specs = (P("dp", None), P("dp", None), P())
    out_specs = (P(), P("dp", None), P("dp", None), P())
    return jax.shard_map(
        on_device, mesh=mesh, in_specs=in_specs, out_specs=out_specs, check_vma=False
    )
```

```python
import functools

import jax
import jax.numpy as jnp
from jax import lax
from jax.experimental import pallas as pl
from jax.experimental.pallas import tpu as pltpu
from jax.sharding import PartitionSpec as P

WIN = 8
BOTH = (0, 1)
LIMIT = 10 * 1024 * 1024
TILE = 256
F32 = jnp.float32
BF16 = jnp.bfloat16
VMEM = pl.BlockSpec(memory_space=pltpu.VMEM)
SMEM = pl.BlockSpec(memory_space=pltpu.SMEM)
ANY = pl.BlockSpec(memory_space=pl.ANY)


def shift(value, steps, cores=BOTH):
    count = lax.axis_size("dp")
    pairs = [(s, (s + steps) % count) for s in range(count) if s % 2 in cores]
    return lax.ppermute(value, "dp", pairs)


def along(value, sign):
    count = lax.axis_size("dp")
    pairs = [(s, (s + sign * (2 + 2 * (s % 2))) % count) for s in range(count)]
    return lax.ppermute(value, "dp", pairs)


def swap(value, bit=1):
    count = lax.axis_size("dp")
    return lax.ppermute(value, "dp", [(s, s ^ bit) for s in range(count)])


def after(value, *done):
    return lax.optimization_barrier((value, done))[0]


def call(kernel, name, micros, outs, args, scratch=(), alias=None, in_hbm=(), out_hbm=()):
    return pl.pallas_call(
        kernel,
        name=name,
        out_shape=[jax.ShapeDtypeStruct(s, d) for s, d in outs],
        in_specs=[SMEM] + [ANY if k in in_hbm else VMEM for k in range(1, len(args))],
        out_specs=[ANY if k in out_hbm else VMEM for k in range(len(outs))],
        scratch_shapes=[pltpu.VMEM(*x) if isinstance(x, tuple) else x for x in scratch],
        compiler_params=pltpu.CompilerParams(vmem_limit_bytes=LIMIT),
        input_output_aliases=alias or {},
        cost_estimate=pl.CostEstimate(
            flops=int(micros * 1.15e9), bytes_accessed=1, transcendentals=0
        ),
    )(*args)


def dot_nt(a, b):
    return lax.dot_general(a, b, (((1,), (1,)), ((), ())), preferred_element_type=F32)


def dot_nn(a, b):
    return lax.dot_general(a, b, (((1,), (0,)), ((), ())), preferred_element_type=F32)


def two(x):
    h = x.astype(BF16)
    return h, (x - h.astype(F32)).astype(BF16)


def three(x):
    h = x.astype(BF16)
    r = x - h.astype(F32)
    m = r.astype(BF16)
    return h, m, (r - m.astype(F32)).astype(BF16)


def scores(a, b):
    (ah, am, al), (bh, bm, bl) = a, b
    small = dot_nt(ah, bl) + dot_nt(al, bh) + dot_nt(am, bm)
    return (small + (dot_nt(ah, bm) + dot_nt(am, bh))) + dot_nt(ah, bh)


def put_three(x, h, m, l):
    h[...], m[...], l[...] = three(x)


def take(refs, rows=slice(None)):
    return tuple(r[rows] for r in refs)


def column(v):
    return jnp.transpose(jnp.broadcast_to(v, (8, v.shape[1])))[:, :1]


def row(v):
    return jnp.transpose(jnp.broadcast_to(v, (v.shape[0], 128)))[:1]


def stat(tops, sums, means):
    top = functools.reduce(jnp.maximum, tops)
    total = sum(jnp.exp(t - top) * s for t, s in zip(tops, sums))
    mean = sum(jnp.exp(t - top) * m for t, m in zip(tops, means))
    return top + jnp.log(total), mean / total


def merge(parts):
    return stat([p[0] for p in parts], [1.0] * len(parts), [p[1] for p in parts])


def lse(blocks, axis):
    top = functools.reduce(
        jnp.maximum, [jnp.max(b, axis=axis, keepdims=True) for b in blocks]
    )
    total, mean = 0.0, 0.0
    for b in blocks:
        e = jnp.exp(b - top)
        total += jnp.sum(e, axis=axis, keepdims=True)
        mean += jnp.sum(e * b, axis=axis, keepdims=True)
    return top + jnp.log(total), mean / total


def own_kernel(s, a0, a1, b0, h, m, l, out, bh, bm, bl):
    n = a0.shape[0]
    for k, a in enumerate((a0, a1)):
        r = pl.ds(k * n, n)
        h[r], m[r], l[r] = three(a[...])
    put_three(b0[...], bh, bm, bl)
    out[...] = s[0] * scores(take((h, m, l)), take((bh, bm, bl)))


def near_kernel(s, h, m, l, b0, bm, bp, lp, lm, blocks_h, blocks_l, *parts):
    n = b0.shape[0]
    r = pl.ds(0, n)
    blocks_h[r], blocks_l[r] = two(b0[...])
    for k, (block, out) in enumerate(((bp, lp), (bm, lm))):
        put_three(block[...], *parts)
        r = pl.ds((k + 2) * n, n)
        blocks_h[r], blocks_l[r] = parts[0][...], parts[1][...]
        out[...] = s[0] * scores(take((h, m, l)), take(parts))


def near_stats_kernel(s, l0, lp, lm, top, mean, diag):
    n = l0.shape[1]
    t, m = lse([l0[...], lp[...], lm[...]], 1)
    top[...] = jnp.broadcast_to(t, top.shape)
    mean[...] = jnp.broadcast_to(m, mean.shape)
    i = lax.broadcasted_iota(jnp.int32, (n, n), 0)
    j = lax.broadcasted_iota(jnp.int32, (n, n), 1)
    diag[...] = jnp.sum(jnp.where(i == j, l0[0:n, :], 0.0), axis=0, keepdims=True)


def put_far(s, parts, k, block, lf, blocks_h, blocks_l, split):
    n = block.shape[0]
    put_three(block, *split)
    r = pl.ds((1 + 3 * k) * n, n)
    blocks_h[r], blocks_l[r] = split[0][...], split[1][...]
    r = pl.ds(k * n, n)
    lf[r, :] = s[0] * scores(take(parts, r), take(split))


def put_rows(k, top, mean, lf, out, at):
    n = lf.shape[1]
    r = pl.ds(k * n, n)
    t, m = merge([(top[r, :1], mean[r, :1]), lse([lf[r, :]], 1)])
    out[at : at + 1, :] = row(t)
    out[at + 1 : at + 2, :] = row(m)


def text_far_kernel(s, xh, xm, xl, a, b, top, mean, old_h, old_l, lf, rows_out, blocks_h, blocks_l, *split):
    first = s[1] == 0.0
    for k, block in ((0, a[...]), (1, jnp.where(first, a[...], b[...]))):
        put_far(s, (xh, xm, xl), k, block, lf, blocks_h, blocks_l, split)
        put_rows(k, top, mean, lf, rows_out, 2 * k)


def image_behind_kernel(s, yh, ym, yl, block, top, mean, old_h, old_l, image_rows, diag, lf, out, blocks_h, blocks_l, *split):
    n = block.shape[0]
    put_far(s, (yh, ym, yl), 0, block[...], lf, blocks_h, blocks_l, split)
    put_rows(0, top, mean, lf, out, 4)
    out[0:4, :] = image_rows[...]
    out[8:9, :] = diag[...]
    out[9:16, :] = jnp.zeros((7, n), F32)

    @pl.when(s[1] != 0.0)
    def _():
        put_far(s, (yh, ym, yl), 1, block[...], lf, blocks_h, blocks_l, split)
        put_rows(1, top, mean, lf, out, 6)


def image_ahead_kernel(s, yh, ym, yl, block, top, mean, old_h, old_l, old_lf, old, lf, out, blocks_h, blocks_l, *split):
    @pl.when(s[1] == 0.0)
    def _():
        put_far(s, (yh, ym, yl), 1, block[...], lf, blocks_h, blocks_l, split)
        put_rows(1, top, mean, lf, out, 6)


def merge_kernel(s, mine, got, out):
    pair = lambda ref, k: (ref[k : k + 1, :], ref[k + 1 : k + 2, :])
    n = out.shape[1]
    terms = []
    for k, ref, j in ((0, mine, 2), (2, got, 0)):
        row_stat = merge([pair(mine, k), pair(got, j)])
        col_stat = merge([pair(mine, k + 4), pair(got, j + 4)])
        out[k : k + 1, :] = row_stat[0]
        out[k + 1 : k + 2, :] = col_stat[0]
        diag = ref[8:9, :]
        terms.append(
            [
                jnp.sum(r + c - 2.0 * diag, axis=1, keepdims=True)
                for r, c in zip(row_stat, col_stat)
            ]
        )
    for k in range(2):
        both = terms[0][k] + terms[1][k]
        out[4 + k : 5 + k, :] = jnp.broadcast_to(both, (1, n))
    out[6:8, :] = jnp.zeros((2, n), F32)


def sort_kernel(s, own, v, vs, u, us, out):
    first = s[1] == 0.0
    for k, (a, b) in enumerate(((u, us), (v, vs))):
        out[2 * k : 2 * k + 2, :] = jnp.where(first, a[0:2, :], b[2:4, :])
        out[2 * k + 4 : 2 * k + 6, :] = jnp.where(first, b[2:4, :], a[0:2, :])


def pair_kernel(s, own, mate, out):
    out[...] = jnp.zeros_like(out)
    out[0:2, :] = own[4:6, :128] + mate[4:6, :128]


def paired(values):
    if len(values) == 1:
        return values[0]
    return paired([a + b for a, b in zip(values[::2], values[1::2])])


def sum_kernel(s, *refs):
    refs[-1][...] = paired([r[...] for r in refs[:-1]])


def last_kernel(s, *refs):
    *terms, loss, scale_grad = refs
    total = paired([t[...] for t in terms]) * (1.0 / s[2])
    loss[...] = total[0:1, 0:1]
    scale_grad[...] = total[1:2, 0:1] / s[0]


def weigh(x, side, m):
    return jnp.exp(x - side) + jnp.exp(x - m)


def less_twice_eye(w):
    i = lax.broadcasted_iota(jnp.int32, w.shape, 0)
    j = lax.broadcasted_iota(jnp.int32, w.shape, 1)
    return jnp.where(i == j, w - 2.0, w)


def put_weights(text, sib, s, own, lses, lp, lm, lf, wh, wl):
    n = lp.shape[1]
    first = s[1] == 0.0
    rows = pl.ds(n if sib else 0, n)
    k = (2 if sib else 0) + (1 if text else 0)
    side = column(own[k : k + 1, :])
    k = 0 if text else 1
    m2, p2, behind, ahead = (lses[j + k : j + k + 1, :] for j in (0, 2, 4, 6))
    if sib:
        far = jnp.where(first, ahead, behind)
    else:
        far = behind if text else ahead
    near = [(lp, m2), (lm, p2)]
    pieces = near + [(lf, far)] if sib else [(lf, far)] + near
    for k, (v, m) in enumerate(pieces):
        w = weigh(v[rows, :], side, m)
        at = pl.ds(k * n, n)
        wh[:, at], wl[:, at] = two(w)


def tile_grads(wh, wl, bh, bl, rows, d):
    h, l = wh[...], wl[...]
    return (dot_nn(h, bl[rows, d]) + dot_nn(l, bh[rows, d])) + dot_nn(h, bh[rows, d])


def own_blocks_kernel(s, own, l0, v0, th, tl, ih, il, image_out, text_out, wh, wl):
    n = l0.shape[1]
    for text, x, bh, bl, out in ((0, l0, th, tl, image_out), (1, v0, ih, il, text_out)):
        side = jnp.concatenate(
            [column(own[text : text + 1, :]), column(own[text + 2 : text + 3, :])]
        )
        w = weigh(x[...], side, own[1 - text : 2 - text, :])
        wh[...], wl[...] = two(less_twice_eye(w))
        for k in range(out.shape[1] // TILE):
            d = pl.ds(k * TILE, TILE)
            out[:, d] = tile_grads(wh, wl, bh, bl, pl.ds(0, n), d)


def share_kernel(text, *refs):
    *args, bh, bl, first, out, wh, wl = refs
    put_weights(text, True, *args, wh, wl)
    n = out.shape[0]
    for k in range(out.shape[1] // TILE):
        d = pl.ds(k * TILE, TILE)
        total = tile_grads(wh, wl, bh, bl, pl.ds(2 * n, 3 * n), d)
        out[:, d] = total + first[n:, d]


def grads_kernel(text, *refs):
    *args, bh, bl, first, share, out, wh, wl, done, sem = refs
    put_weights(text, False, *args, wh, wl)
    n = share.shape[0]
    factor = 0.5 * args[0][0]
    copies = []
    for k in range(out.shape[1] // TILE):
        d = pl.ds(k * TILE, TILE)
        total = tile_grads(wh, wl, bh, bl, pl.ds(n, 3 * n), d)
        done[:, d] = factor * ((total + first[0:n, d]) + share[:, d])
        copies.append(pltpu.make_async_copy(done.at[:, d], out.at[:, d], sem.at[k]))
        copies[-1].start()
    for copy in copies:
        copy.wait()


def on_device(image, text, scale):
    n, depth = image.shape
    device = lax.axis_index("dp")
    core = (device % 2).astype(F32)
    s = jnp.stack([scale, core, jnp.float32(2 * n * lax.axis_size("dp"))])
    block = ((n, depth), F32)
    both = ((2 * n, n), F32)
    part = ((2 * n, depth), BF16)
    wide = ((2 * n, 128), F32)
    four, line = ((4, n), F32), ((1, n), F32)
    split = [((n, depth), BF16)] * 3

    t_p, t_m = shift(text, 2), shift(text, -2)
    i_s, t_s = swap(image), swap(text)
    i_p, i_m = shift(image, 2), shift(image, -2)
    args = s, after(image, t_s), i_s, text
    *x, l0 = call(own_kernel, "text_own", 3.7, [part] * 3 + [both], args, split)
    args = s, after(text, l0), t_s, image
    *y, v0 = call(own_kernel, "image_own", 3.7, [part] * 3 + [both], args, split)
    t_p, t_m = after(t_p, v0), after(t_m, v0)
    t_pp, t_mm = shift(t_p, 2, (1,)), shift(t_m, -2)
    five = [((5 * n, depth), BF16)] * 2
    near_outs = [both] * 2 + five
    args = s, *x, text, t_m, t_p
    lp, lm, *t_parts = call(near_kernel, "text_near", 4.8, near_outs, args, split)
    args = s, l0, lp, lm
    top, mean, diag = call(near_stats_kernel, "text_stats", 1.8, [wide] * 2 + [line], args)
    i_p, i_m = after(i_p, top), after(i_m, top)
    i_pp, i_mm = shift(i_p, 2), shift(i_m, -2, (0,))
    args = s, *y, image, i_m, i_p
    vp, vm, *i_parts = call(near_kernel, "image_near", 4.8, near_outs, args, split)
    args = s, v0, vp, vm
    i_top, i_mean, _ = call(near_stats_kernel, "image_stats", 1.8, [wide] * 2 + [line], args)
    args = s, *x, after(t_mm, i_top), t_pp, top, mean, *t_parts
    outs = [both, four] + five
    kept = {8: 2, 9: 3}
    lf, image_rows, *t_parts = call(text_far_kernel, "text_far", 4.0, outs, args, split, kept)
    args = s, *y, after(i_pp, lf), i_top, i_mean, *i_parts, image_rows, diag
    outs = [both, ((16, n), F32)] + five
    kept = {7: 2, 8: 3}
    vf, mine, *i_parts = call(image_behind_kernel, "image_behind", 3.0, outs, args, split, kept)
    args = s, *y, i_mm, i_top, i_mean, *i_parts, vf, mine
    kept = {7: 2, 8: 3, 9: 0, 10: 1}
    vf, mine, *i_parts = call(image_ahead_kernel, "image_ahead", 2.0, outs, args, split, kept)

    got = swap(mine)
    (own,) = call(merge_kernel, "merge", 0.6, [((8, n), F32)], (s, mine, got))
    u, v = along(own, 1), along(own, -1)
    terms = [((8, 128), F32)]
    (parts,) = call(pair_kernel, "pair", 0.5, terms, (s, own, swap(own, 16)))

    def add(parts, bits, *done):
        args = s, after(parts, *done), *(swap(parts, b) for b in bits)
        return call(sum_kernel, "sum", 0.5, terms, args)[0]

    parts = add(parts, (32,))
    args = s, own, l0, v0, *t_parts, *i_parts
    firsts = [((2 * n, depth), F32)] * 2
    w_part = [((2 * n, n), BF16)] * 2
    image_first, text_first = call(own_blocks_kernel, "own_blocks", 3.0, firsts, args, w_part)
    args = s, after(own, parts), v, swap(after(v, image_first)), u, swap(u)
    (lses,) = call(sort_kernel, "sort", 0.5, [((8, n), F32)], args)

    image_args = lp, lm, lf, *t_parts, image_first
    text_args = vp, vm, vf, *i_parts, text_first
    weights = [((n, 3 * n), BF16)] * 2
    final = [block, pltpu.SemaphoreType.DMA((depth // TILE,))]
    kernel = functools.partial(share_kernel, False)
    (share,) = call(kernel, "image_share", 3.1, [block], (s, own, lses, *image_args), weights)
    parts = add(parts, (2,), share)
    image_share = swap(after(share, parts))
    kernel = functools.partial(share_kernel, True)
    args = s, after(own, parts), lses, *text_args
    (share,) = call(kernel, "text_share", 3.1, [block], args, weights)
    parts = add(parts, (64, 128, 192), share)
    text_share = swap(after(share, parts))

    far_part = swap(parts, 8)
    kernel = functools.partial(grads_kernel, False)
    args = s, after(own, parts), lses, *image_args, image_share
    final = weights + final
    (image_grad,) = call(kernel, "image_grads", 3.9, [block], args, final, out_hbm=(0,))
    args = s, after(parts, image_grad), far_part
    (parts,) = call(sum_kernel, "sum", 0.5, terms, args)
    last_part = swap(parts, 4)
    kernel = functools.partial(grads_kernel, True)
    args = s, after(own, parts), lses, *text_args, text_share
    (text_grad,) = call(kernel, "text_grads", 3.9, [block], args, final, out_hbm=(0,))
    args = s, after(parts, text_grad), last_part
    loss, scale_grad = call(last_kernel, "last", 0.5, [((1, 1), F32)] * 2, args)
    return (loss.reshape(()), image_grad, text_grad, scale_grad.reshape(()))


def solution(mesh):
    in_specs = (P("dp", None), P("dp", None), P())
    out_specs = (P(), P("dp", None), P("dp", None), P())
    return jax.shard_map(
        on_device, mesh=mesh, in_specs=in_specs, out_specs=out_specs, check_vma=False
    )
```
